32 devices in a mesh: group: 2 (over x), tile: 8 (over z, y), comp: 2 (over core).
Axes of the slice: x: 2, y: 2, z: 4, core: 2. Of those that a mesh axis runs over, the one named last changes fastest.
Arguments:
- action: float32 [50, 36, 64, 128], P('comp', None, ('group', 'tile')), parts along dimension 2, may hold values from 0.05 to 1
- sea_mask: int32 [64, 128], P(('group', 'tile')), parts along dimension 0, may hold values from 0 to 1, as said below
- order: int32 [16, 384], P(('group', 'tile')), parts along dimension 0, may hold values from 0 to 511, as said below
- grad_x: float32 [64, 128], P(('group', 'tile')), parts along dimension 0, may hold values from -0.5 to 0.5
- grad_y: float32 [64, 128], P(('group', 'tile')), parts along dimension 0, may hold values from -0.5 to 0.5
- shift_rate: float32 [64, 128], P(('group', 'tile')), parts along dimension 0, may hold values from -0.8 to 0.8
- wind_speed: float32 [64, 128], P(('group', 'tile')), parts along dimension 0, may hold values from 0.5 to 2
- wind_dir: float32 [64, 128], P(('group', 'tile')), parts along dimension 0, may hold values from -3.140625 to 3.140625
Outputs:
- sea_spectra: float32 [50, 36, 6144], P(None, None, ('group', 'tile', 'comp')), parts along dimension 2
The draws below stay inside these ranges and needn't reach their ends.
There are 2 independent parts, one for each index of `group`. The reference program is written for one: setup_inputs(seed, part) draws one part's arguments, and reference() takes and returns one part's arrays. A program takes and returns all parts, laid end to end along the dimension named above; each array names one. Nothing has to cross between parts.
Inputs may be any that keep to these rules, and one draw needn't show every extreme that they name: `order`: row t lists 384 distinct cells of tile t as r * 128 + c (r the row within the tile): all sea cells of the tile first, then land cells. A tile has at most 384 sea cells and some tile has exactly 384. `sea_mask`: agrees with order.
All inputs are finite; a program needn't handle non-finite values.
Results may differ from the reference program's by a relative error of at most 0.0003.
Values sent between devices are 32-bit elements; how exact they have to be, the bound alone decides.
A program may use at most 64 MiB of HBM per device.

```python
import math
import jax
import jax.numpy as jnp
from jax import lax

NF = 50
ND = 36
TX = 4
NY = 128
PAIR = 24
SEA_MAX = 384
NX = 32
SEA_SLOT_COUNT = 3072
N_TILE = 8
N_COMP = 2


def shuffle(subkey):
    return jax.random.permutation(subkey, TX * NY)


def sea_layout(key):
    count_key, pick_key, permute_key = jax.random.split(key, 3)
    cells = TX * NY
    counts = jax.random.randint(count_key, (N_TILE,), SEA_MAX // 4, SEA_MAX + 1)
    busiest_slab = jax.random.randint(pick_key, (), 0, N_TILE)
    counts = jnp.where(jnp.arange(N_TILE) == busiest_slab, SEA_MAX, counts)
    perms = jax.vmap(shuffle)(jax.random.split(permute_key, N_TILE)).astype(jnp.int32)
    ranked = (jnp.arange(cells)[None, :] < counts[:, None]).astype(jnp.int32)
    flags = jnp.zeros((N_TILE, cells), jnp.int32).at[jnp.arange(N_TILE)[:, None], perms].set(ranked)
    return (flags, perms)


def draw_sea_mask(key, part):
    flags, perms = sea_layout(key)
    return flags.reshape(N_TILE * TX, NY)


def draw_order(key, part):
    flags, perms = sea_layout(key)
    return perms[:, :SEA_MAX]


def level_of(stream_key, dims, shards, least, high):
    def one(position, blocks):
        heights = jax.random.uniform(jax.random.fold_in(jax.random.fold_in(stream_key, 6), position), (blocks,), jnp.float32, least / len(shards), high / len(shards))
        return jnp.repeat(jnp.exp(heights), dims[position] // blocks).reshape((-1,) + (1,) * (len(dims) - position - 1))

    gain = one(*shards[0])
    for cut in shards[1:]:
        gain = gain * one(*cut)
    return gain


def setup_inputs(seed: int = 0, part: int = 0) -> dict:
    key_of = jax.random.split(jax.random.key(seed), 9)
    part_splits = jax.random.split(jax.random.fold_in(key_of[8], part), 9)
    return {
        "action": jnp.clip(jnp.exp(math.log(1.0) - 2.9957323 * jax.random.uniform(part_splits[0], (NF, ND, NX, NY), jnp.float32) ** level_of(part_splits[0], (NF, ND, NX, NY), ((0, 2), (2, 8)), -0.2, 0.2)), 0.05, 1.0),
        "sea_mask": draw_sea_mask(jax.random.fold_in(jax.random.fold_in(key_of[8], part), 71), part),
        "order": draw_order(jax.random.fold_in(jax.random.fold_in(key_of[8], part), 71), part),
        "grad_x": jnp.clip(jax.random.uniform(part_splits[3], (NX, NY), jnp.float32, -0.5, 0.5) * level_of(part_splits[3], (NX, NY), ((0, 8),), -0.4, 0.0), -0.5, 0.5),
        "grad_y": jnp.clip(jax.random.uniform(part_splits[4], (NX, NY), jnp.float32, -0.5, 0.5) * level_of(part_splits[4], (NX, NY), ((0, 8),), -0.4, 0.0), -0.5, 0.5),
        "shift_rate": jnp.clip(jax.random.uniform(part_splits[5], (NX, NY), jnp.float32, -0.8, 0.8) * level_of(part_splits[5], (NX, NY), ((0, 8),), -0.4, 0.0), -0.8, 0.8),
        "wind_speed": jnp.clip(jnp.exp(math.log(2.0) - 1.3862944 * jax.random.uniform(part_splits[6], (NX, NY), jnp.float32) ** level_of(part_splits[6], (NX, NY), ((0, 8),), -0.2, 0.2)), 0.5, 2.0),
        "wind_dir": jnp.clip(jax.random.uniform(part_splits[7], (NX, NY), jnp.float32, -3.140625, 3.140625), -3.140625, 3.140625),
    }


ratio_step = 1.07
courant_top = 0.8
wind_gain = 0.05
dissipation = 1.0
steep_norm = 0.1
reciprocal_lower_limit = 0.05


def directions(count):
    return (jnp.arange(count).astype(jnp.float32) + 0.5) * (2.0 * jnp.pi / count)


def frequency_scale(first, count, total):
    index = (first + jnp.arange(count)).astype(jnp.float32)
    return ratio_step ** (index - 0.5 * (total - 1))


def courant_scale(first, count):
    index = (first + jnp.arange(count)).astype(jnp.float32)
    return courant_top * ratio_step ** (-index)


def quickest(padded, face_rate, axis):
    size = padded.shape[axis] - 4
    outer_left = lax.slice_in_dim(padded, 0, size + 1, axis=axis)
    left = lax.slice_in_dim(padded, 1, size + 2, axis=axis)
    right = lax.slice_in_dim(padded, 2, size + 3, axis=axis)
    outer_right = lax.slice_in_dim(padded, 3, size + 4, axis=axis)
    bend = jnp.where(face_rate >= 0.0, right - 2.0 * left + outer_left, outer_right - 2.0 * right + left)
    face = 0.5 * (left + right) - 0.5 * face_rate * (right - left) - (1.0 - face_rate * face_rate) / 6.0 * bend
    flux = face_rate * face
    inner = lax.slice_in_dim(padded, 2, size + 2, axis=axis)
    return inner - (lax.slice_in_dim(flux, 1, size + 1, axis=axis) - lax.slice_in_dim(flux, 0, size, axis=axis))


def apply_refraction(spectra, slope_x, slope_y, sines, cosines):
    turning = sines * slope_x - cosines * slope_y
    wrapped = jnp.concatenate([spectra[:, -2:], spectra, spectra[:, :2]], axis=1)
    turn_wrap = jnp.concatenate([turning[:, -1:], turning, turning[:, :1]], axis=1)
    face_rate = 0.5 * (turn_wrap[:, :-1] + turn_wrap[:, 1:])
    return quickest(wrapped, face_rate, 1)


def wind_input(spectra, relative, speed, angle, theta):
    growth = wind_gain * jnp.maximum(speed * relative * jnp.cos(theta - angle) - 1.0, 0.0)
    return spectra * (1.0 + growth)


def frequency_shift(spectra, rate, cosines):
    padded = jnp.pad(spectra, ((2, 2),) + ((0, 0),) * (spectra.ndim - 1))
    return quickest(padded, rate * cosines, 0)


def whitecap(spectra, relative):
    energy = jnp.mean(spectra, axis=(0, 1), keepdims=True)
    inverse = jnp.mean(spectra / relative, axis=(0, 1), keepdims=True)
    mean_freq = energy / jnp.maximum(inverse, reciprocal_lower_limit)
    damping = dissipation * relative ** 2 * energy ** 2 * mean_freq ** 7 / steep_norm ** 2
    return spectra / (1.0 + damping)


def reference(action, sea_mask, order, grad_x, grad_y, shift_rate, wind_speed, wind_dir):
    theta = directions(ND)
    sines = jnp.sin(theta)[None, :, None, None]
    cosines = jnp.cos(theta)[None, :, None, None]
    relative = frequency_scale(0, NF, NF)[:, None, None, None]
    group_speeds = courant_scale(0, NF)[:, None, None, None]
    land = sea_mask.astype(jnp.float32)
    spectra = action * land
    spectra = quickest(jnp.pad(spectra, ((0, 0), (0, 0), (2, 2), (0, 0))), group_speeds * cosines, 2)
    spectra = quickest(jnp.pad(spectra, ((0, 0), (0, 0), (0, 0), (2, 2))), group_speeds * sines, 3) * land
    spectra = apply_refraction(spectra, grad_x[None, None], grad_y[None, None], sines, cosines)
    spectra = wind_input(spectra, relative, wind_speed[None, None], wind_dir[None, None], theta[None, :, None, None])
    devices_all = N_TILE * N_COMP
    column_index = jnp.arange(SEA_SLOT_COUNT).astype(jnp.int32)
    owner = column_index // (N_TILE * PAIR)
    rest = column_index % (N_TILE * PAIR)
    tile_of = rest // PAIR
    slot = (rest % PAIR) * devices_all + owner
    cell = tile_of * (TX * NY) + order[tile_of, slot]
    points = jnp.take(spectra.reshape(NF, ND, NX * NY), cell, axis=2)
    shift = jnp.take(shift_rate.reshape(NX * NY), cell)
    points = frequency_shift(points, shift[None, None, :], jnp.cos(theta)[None, :, None])
    return whitecap(points, frequency_scale(0, NF, NF)[:, None, None])
```

```python
import functools
import math

import jax
import jax.numpy as jnp
import numpy as np
from jax import lax
from jax.experimental import pallas as pl
from jax.experimental.pallas import tpu as pltpu
from jax.sharding import PartitionSpec as P

ratio_step = 1.07
courant_top = 0.8
wind_gain = 0.05
dissipation = 1.0
steep_norm = 0.1
reciprocal_lower_limit = 0.05
LOG_STEP = math.log(ratio_step)
CHUNK = 256
MESH = pl.DeviceIdType.MESH
F32 = jnp.float32
BF16 = jnp.bfloat16


def stencil_weights(rate):
    k = (1.0 - rate * rate) * (1.0 / 6.0)
    kc = k * rate
    left = rate * (0.5 + 0.5 * rate)
    right = rate * (0.5 - 0.5 * rate)
    ahead = rate >= 0.0
    zero = jnp.zeros_like(rate)
    f0 = jnp.where(ahead, -kc, zero)
    f1 = left + jnp.where(ahead, 2.0 * kc, -kc)
    f2 = right + jnp.where(ahead, -kc, 2.0 * kc)
    f3 = jnp.where(ahead, zero, -kc)
    return f0, f1, f2, f3


def cell_weights(lower, upper):
    return (
        lower[0],
        lower[1] - upper[0],
        1.0 + lower[2] - upper[1],
        lower[3] - upper[2],
        -upper[3],
    )


def two_parts(value):
    high = value.astype(BF16)
    return high, (value - high.astype(F32)).astype(BF16)


def kernel(
    shape, x_ref, mask_ref, order_ref, gx_ref, gy_ref, shift_ref, speed_ref, dir_ref, trig_ref,
    out_ref,
    down_out, up_out, down_in, up_in, far_up, far_down, wx_ref, wy_ref, wd_ref, wind_ref, ring_ref,
    aw_ref, hot_ref, send_ref, recv_ref, flat_ref, wf_ref, af_ref,
    halo_send, halo_recv, part_send, part_recv,
):
    tiles, halves, local_f, angles, rows, width, pair, padded, pitch, starts = shape
    groups = len(starts) - 1
    devices_all = tiles * halves
    group, tile, half = lax.axis_index("group"), lax.axis_index("tile"), lax.axis_index("comp")
    me = tile * halves + half
    first = half * local_f
    low = angles // 4
    high = angles - low
    side = angles // 2

    barrier = pltpu.get_barrier_semaphore()

    def greet(step, carry):
        other = lax.rem(me + step, devices_all)
        pl.semaphore_signal(
            barrier, inc=1, device_id=(group, other // halves, lax.rem(other, halves)),
            device_id_type=MESH,
        )
        return carry

    lax.fori_loop(1, devices_all, greet, 0)

    land = mask_ref[...].astype(F32)
    land_rows = [jnp.broadcast_to(land[r : r + 1], (angles, width)) for r in range(rows)]

    def row_of(j, r):
        return x_ref[j, pl.ds(r, angles, stride=rows), :] * land_rows[r]

    def stage(j, carry):
        down_out[j, pl.ds(0, angles), :] = row_of(j, rows - 1)
        second = row_of(j, rows - 2)
        down_out[j, pl.ds(angles, low), :] = second[:low]
        down_out[j, pl.ds(angles + low, low), :] = second[high:]
        up_out[j, pl.ds(0, angles), :] = row_of(j, 0)
        up_out[j, pl.ds(angles, side), :] = row_of(j, 1)[low:high]
        return carry

    lax.fori_loop(0, local_f, stage, 0)
    pl.semaphore_wait(barrier, devices_all - 1)

    def down_copy(g):
        part = pl.ds(starts[g], starts[g + 1] - starts[g])
        return pltpu.make_async_remote_copy(
            src_ref=down_out.at[part], dst_ref=down_in.at[part],
            send_sem=halo_send.at[0, g], recv_sem=halo_recv.at[0, g],
            device_id=(group, lax.rem(tile + 1, tiles), half), device_id_type=MESH,
        )

    def up_copy(g):
        part = pl.ds(starts[g], starts[g + 1] - starts[g])
        return pltpu.make_async_remote_copy(
            src_ref=up_out.at[part], dst_ref=up_in.at[part],
            send_sem=halo_send.at[1, g], recv_sem=halo_recv.at[1, g],
            device_id=(group, lax.rem(tile + tiles - 1, tiles), half), device_id_type=MESH,
        )

    for g in range(groups):
        @pl.when(tile < tiles - 1)
        def _():
            down_copy(g).start()

        @pl.when(tile > 0)
        def _():
            up_copy(g).start()

    @pl.when(tile == 0)
    def _():
        down_in[...] = jnp.zeros_like(down_in)

    @pl.when(tile == tiles - 1)
    def _():
        up_in[...] = jnp.zeros_like(up_in)

    far_up[...] = jnp.zeros_like(far_up)
    far_down[...] = jnp.zeros_like(far_down)
    aw_ref[...] = jnp.zeros_like(aw_ref)
    for r in range(rows):
        aw_ref[pl.ds(local_f * pitch, 1), pl.ds(r * width, width)] = shift_ref[pl.ds(r, 1), :]
    cosines = trig_ref[0, :, :width]
    sines = trig_ref[1, :, :width]
    column = lax.broadcasted_iota(jnp.int32, (angles, width), 1)

    def tables(j, carry):
        index = (first + j).astype(F32)
        speed = courant_top * jnp.exp(jnp.full((1, width), -LOG_STEP, F32) * index)
        flux = stencil_weights(speed * cosines)
        for k, weight in enumerate(cell_weights(flux, flux)):
            wx_ref[j, k] = weight
        flux = stencil_weights(speed * sines)
        for k, weight in enumerate(cell_weights(flux, flux)):
            at = column + (k - 2)
            wy_ref[j, k] = jnp.where((at >= 0) & (at < width), weight, 0.0)
        return carry

    lax.fori_loop(0, local_f, tables, 0)

    wind_cos = jnp.cos(dir_ref[...]) * speed_ref[...]
    wind_sin = jnp.sin(dir_ref[...]) * speed_ref[...]
    for r in range(rows):
        turning = sines * gx_ref[pl.ds(r, 1), :] - cosines * gy_ref[pl.ds(r, 1), :]
        ring_ref[r, pl.ds(1, angles), :] = turning
        ring_ref[r, pl.ds(0, 1), :] = turning[angles - 1 :]
        ring_ref[r, pl.ds(angles + 1, 1), :] = turning[:1]
        lower = stencil_weights(0.5 * (ring_ref[r, pl.ds(0, angles), :] + turning))
        upper = stencil_weights(0.5 * (turning + ring_ref[r, pl.ds(2, angles), :]))
        for k, weight in enumerate(cell_weights(lower, upper)):
            wd_ref[r, k] = weight * land_rows[r]
        wind_ref[r] = cosines * wind_cos[r : r + 1] + sines * wind_sin[r : r + 1]

    slots = order_ref.shape[1]
    cells = rows * width
    at_cell = lax.broadcasted_iota(jnp.int32, (cells, slots), 0) == order_ref[...]
    at_cell = jnp.where(at_cell, 1.0, 0.0).astype(BF16)
    slot = lax.broadcasted_iota(jnp.int32, (devices_all * padded, slots), 1)
    line = lax.broadcasted_iota(jnp.int32, (devices_all * padded, slots), 0)
    shifted = slot.dtype.type(devices_all.bit_length() - 1)
    place = (slot & (devices_all - 1)) * padded + lax.shift_right_logical(
        slot, jnp.full(slot.shape, shifted, jnp.int32)
    )
    pick = jnp.where(line == place, 1.0, 0.0).astype(BF16)
    hot_ref[...] = lax.dot_general(
        pick, at_cell, (((1,), (1,)), ((), ())), preferred_element_type=F32
    ).astype(BF16)

    def advance(j, carry):
        a = [row_of(j, r) for r in range(rows)]
        up1 = down_in[j, pl.ds(0, angles), :]
        far_up[pl.ds(0, low), :] = down_in[j, pl.ds(angles, low), :]
        far_up[pl.ds(high, low), :] = down_in[j, pl.ds(angles + low, low), :]
        dn1 = up_in[j, pl.ds(0, angles), :]
        far_down[pl.ds(low, side), :] = up_in[j, pl.ds(angles, side), :]
        line_of = [far_up[...], up1, *a, dn1, far_down[...]]
        relative = jnp.exp(
            jnp.full((1, width), LOG_STEP, F32)
            * ((first + j).astype(F32) - 0.5 * (local_f * halves - 1))
        )
        for r in range(rows):
            ax = line_of[r] * wx_ref[j, 0]
            for k in range(1, 5):
                ax = ax + line_of[r + k] * wx_ref[j, k]
            ay = ax * wy_ref[j, 2]
            for k in (0, 1, 3, 4):
                ay = ay + pltpu.roll(ax, (2 - k) % width, 1) * wy_ref[j, k]
            ring_ref[r, pl.ds(2, angles), :] = ay
            ring_ref[r, pl.ds(0, 2), :] = ay[angles - 2 :]
            ring_ref[r, pl.ds(angles + 2, 2), :] = ay[:2]
            ar = ay * wd_ref[r, 2]
            for k in (0, 1, 3, 4):
                ar = ar + ring_ref[r, pl.ds(k, angles), :] * wd_ref[r, k]
            growth = 1.0 + wind_gain * jnp.maximum(wind_ref[r] * relative - 1.0, 0.0)
            aw_ref[pl.ds(pl.multiple_of(j * pitch, 8), angles), pl.ds(r * width, width)] = (
                ar * growth
            )
        return carry

    mine = pl.ds(pl.multiple_of(tile * padded, 8), padded)
    for g in range(groups):
        @pl.when(tile > 0)
        def _():
            down_copy(g).wait_recv()

        @pl.when(tile < tiles - 1)
        def _():
            up_copy(g).wait_recv()

        lax.fori_loop(starts[g], starts[g + 1], advance, 0)
        total = None
        for part in two_parts(aw_ref[pl.ds(g * CHUNK, CHUNK), :]):
            term = lax.dot_general(
                hot_ref[...], part, (((1,), (1,)), ((), ())), preferred_element_type=F32
            )
            total = term if total is None else total + term
        send_ref[g] = total

        def send(step, carry):
            other = lax.rem(me + step, devices_all)
            theirs = pl.ds(pl.multiple_of(other * padded, 8), padded)
            pltpu.make_async_remote_copy(
                src_ref=send_ref.at[g, theirs], dst_ref=recv_ref.at[g, half, mine],
                send_sem=part_send.at[g], recv_sem=part_recv.at[g],
                device_id=(group, other // halves, lax.rem(other, halves)), device_id_type=MESH,
            ).start()
            return carry

        lax.fori_loop(1, devices_all, send, 0)
        own = pl.ds(pl.multiple_of(me * padded, 8), padded)
        pltpu.make_async_copy(
            send_ref.at[g, own], recv_ref.at[g, half, mine], part_recv.at[g]
        ).start()

    points = tiles * pair
    for g in range(groups):
        pltpu.make_async_copy(recv_ref.at[g], recv_ref.at[g], part_recv.at[g]).wait()
        for h in range(halves):
            turned = jnp.transpose(recv_ref[g, h])
            if padded != pair:
                line = lax.broadcasted_iota(jnp.int32, (tiles * padded, points), 0)
                slot = lax.broadcasted_iota(jnp.int32, (tiles * padded, points), 1)
                tile_of = lax.div(slot, jnp.full(slot.shape, pair, jnp.int32))
                keep = jnp.where(line == slot + tile_of * (padded - pair), 1.0, 0.0).astype(BF16)
                turned = sum(
                    jnp.dot(part, keep, preferred_element_type=F32) for part in two_parts(turned)
                )
            flat_ref[h, pl.ds(g * CHUNK, CHUNK), :] = turned

    total_f = local_f * halves
    rate = flat_ref[0, pl.ds(local_f * pitch, 1), :] * trig_ref[0, :, :points]
    flux = stencil_weights(rate)
    for k, weight in enumerate(cell_weights(flux, flux)):
        wf_ref[k] = weight
    af_ref[pl.ds(0, 2)] = jnp.zeros((2, angles, points), F32)
    af_ref[pl.ds(total_f + 2, 2)] = jnp.zeros((2, angles, points), F32)
    for h in range(halves):
        def spread(j, carry):
            af_ref[2 + h * local_f + j] = flat_ref[
                h, pl.ds(pl.multiple_of(j * pitch, 8), angles), :
            ]
            return carry

        lax.fori_loop(0, local_f, spread, 0)

    def relative_at(j):
        return jnp.exp(
            jnp.full((1, points), LOG_STEP, F32) * (j.astype(F32) - 0.5 * (total_f - 1))
        )

    def shift(j, carry):
        energy, inverse = carry
        af = af_ref[j] * wf_ref[0]
        for k in range(1, 5):
            af = af + af_ref[j + k] * wf_ref[k]
        out_ref[j] = af
        return energy + af, inverse + af * (1.0 / relative_at(j))

    zero = jnp.zeros((angles, points), F32)
    energy, inverse = lax.fori_loop(0, total_f, shift, (zero, zero))
    scale = 1.0 / (total_f * angles)
    energy = jnp.sum(energy, axis=0, keepdims=True) * scale
    inverse = jnp.sum(inverse, axis=0, keepdims=True) * scale
    mean_freq = energy / jnp.maximum(inverse, reciprocal_lower_limit)
    square = mean_freq * mean_freq
    steep = energy * energy * (square * square * square * mean_freq) * (
        dissipation / steep_norm**2
    )

    def damp(j, carry):
        relative = relative_at(j)
        out_ref[j] = out_ref[j] * (1.0 / (1.0 + relative * relative * steep))
        return carry

    lax.fori_loop(0, total_f, damp, 0)

    for g in range(groups):
        @pl.when(tile < tiles - 1)
        def _():
            down_copy(g).wait_send()

        @pl.when(tile > 0)
        def _():
            up_copy(g).wait_send()

        sent = send_ref.at[g, pl.ds(0, (devices_all - 1) * padded)]
        pltpu.make_async_copy(sent, sent, part_send.at[g]).wait()


def on_device(action, sea_mask, order, grad_x, grad_y, shift_rate, wind_speed, wind_dir):
    tiles = lax.axis_size("tile")
    halves = lax.axis_size("comp")
    local_f, angles, rows, width = action.shape
    total_f = local_f * halves
    devices_all = tiles * halves
    pair = order.shape[1] // devices_all
    padded = -(-pair // 8) * 8
    points = tiles * pair
    pitch = -(-angles // 8) * 8
    groups = -(-(local_f * pitch + 1) // CHUNK)
    starts = tuple(min(-(-g * CHUNK // pitch), local_f) for g in range(groups)) + (local_f,)
    shape = (tiles, halves, local_f, angles, rows, width, pair, padded, pitch, starts)
    theta = (np.arange(angles) + 0.5) * (2.0 * np.pi / angles)
    trig = np.stack([np.cos(theta), np.sin(theta)]).astype(np.float32)
    trig = jnp.broadcast_to(jnp.asarray(trig)[:, :, None], (2, angles, max(points, width)))
    message = -(-(angles + angles // 2) // 8) * 8
    halo = pltpu.VMEM((local_f, message, width), F32)
    vmem = pl.BlockSpec(memory_space=pltpu.VMEM)
    return pl.pallas_call(
        functools.partial(kernel, shape),
        out_shape=jax.ShapeDtypeStruct((total_f, angles, points), F32),
        in_specs=[vmem] * 9,
        out_specs=vmem,
        scratch_shapes=[
            halo, halo, halo, halo,
            pltpu.VMEM((angles, width), F32),
            pltpu.VMEM((angles, width), F32),
            pltpu.VMEM((local_f, 5, angles, width), F32),
            pltpu.VMEM((local_f, 5, angles, width), F32),
            pltpu.VMEM((rows, 5, angles, width), F32),
            pltpu.VMEM((rows, angles, width), F32),
            pltpu.VMEM((rows, angles + 4, width), F32),
            pltpu.VMEM((groups * CHUNK, rows * width), F32),
            pltpu.VMEM((devices_all * padded, rows * width), BF16),
            pltpu.VMEM((groups, devices_all * padded, CHUNK), F32),
            pltpu.VMEM((groups, halves, tiles * padded, CHUNK), F32),
            pltpu.VMEM((halves, groups * CHUNK, points), F32),
            pltpu.VMEM((5, angles, points), F32),
            pltpu.VMEM((total_f + 4, angles, points), F32),
            pltpu.SemaphoreType.DMA((2, groups)),
            pltpu.SemaphoreType.DMA((2, groups)),
            pltpu.SemaphoreType.DMA((groups,)),
            pltpu.SemaphoreType.DMA((groups,)),
        ],
        compiler_params=pltpu.CompilerParams(
            collective_id=0, has_side_effects=True, vmem_limit_bytes=48 * 1024 * 1024
        ),
    )(
        action.reshape(local_f, angles * rows, width), sea_mask, order, grad_x, grad_y,
        shift_rate, wind_speed, wind_dir, trig,
    )


def solution(mesh):
    return jax.shard_map(
        on_device,
        mesh=mesh,
        in_specs=(
            P("comp", None, ("group", "tile"), None),
            P(("group", "tile"), None),
            P(("group", "tile"), None),
            P(("group", "tile"), None),
            P(("group", "tile"), None),
            P(("group", "tile"), None),
            P(("group", "tile"), None),
            P(("group", "tile"), None),
        ),
        out_specs=P(None, None, ("group", "tile", "comp")),
        check_vma=False,
    )
```

```python
import functools
import math

import jax
import jax.numpy as jnp
import numpy as np
from jax import lax
from jax.experimental import pallas as pl
from jax.experimental.pallas import tpu as pltpu
from jax.sharding import PartitionSpec as P

ratio_step = 1.07
courant_top = 0.8
wind_gain = 0.05
dissipation = 1.0
steep_norm = 0.1
reciprocal_lower_limit = 0.05
LOG_STEP = math.log(ratio_step)
CHUNK = 128
MESH = pl.DeviceIdType.MESH
F32 = jnp.float32
BF16 = jnp.bfloat16


def stencil_weights(rate):
    k = (1.0 - rate * rate) * (1.0 / 6.0)
    kc = k * rate
    left = rate * (0.5 + 0.5 * rate)
    right = rate * (0.5 - 0.5 * rate)
    ahead = rate >= 0.0
    zero = jnp.zeros_like(rate)
    f0 = jnp.where(ahead, -kc, zero)
    f1 = left + jnp.where(ahead, 2.0 * kc, -kc)
    f2 = right + jnp.where(ahead, -kc, 2.0 * kc)
    f3 = jnp.where(ahead, zero, -kc)
    return f0, f1, f2, f3


def cell_weights(lower, upper):
    return (
        lower[0],
        lower[1] - upper[0],
        1.0 + lower[2] - upper[1],
        lower[3] - upper[2],
        -upper[3],
    )


def two_parts(value):
    high = value.astype(BF16)
    return high, (value - high.astype(F32)).astype(BF16)


def kernel(
    shape, x_hbm, mask_hbm, order_hbm, gx_hbm, gy_hbm, shift_hbm, speed_hbm, dir_hbm, trig_hbm,
    out_ref, steep_ref,
    x_ref, mask_ref, order_ref, gx_ref, gy_ref, shift_ref, speed_ref, dir_ref, trig_ref,
    down_out, up_out, down_in, up_in, far_up, far_down, wx_ref, wy_ref, wd_ref, wind_ref, ring_ref,
    aw_ref, hot_ref, send_ref, recv_ref, wf_ref, af_ref,
    x_sem, small_sem, halo_send, halo_recv, part_send, part_recv,
):
    tiles, halves, local_f, angles, rows, width, pair, padded, pitch, starts = shape
    groups = len(starts) - 1
    devices_all = tiles * halves
    group, tile, half = lax.axis_index("group"), lax.axis_index("tile"), lax.axis_index("comp")
    me = tile * halves + half
    first = half * local_f
    low = angles // 4
    high = angles - low
    side = angles // 2

    small = [
        pltpu.make_async_copy(source, target, small_sem.at[i])
        for i, (source, target) in enumerate([
            (mask_hbm, mask_ref), (order_hbm, order_ref), (gx_hbm, gx_ref), (gy_hbm, gy_ref),
            (shift_hbm, shift_ref), (speed_hbm, speed_ref), (dir_hbm, dir_ref),
            (trig_hbm, trig_ref),
        ])
    ]

    def load(g):
        part = pl.ds(starts[g], starts[g + 1] - starts[g])
        return pltpu.make_async_copy(x_hbm.at[part], x_ref.at[part], x_sem.at[g])

    small[0].start()
    for g in range(groups):
        load(g).start()
    for copy in small[1:]:
        copy.start()

    barrier = pltpu.get_barrier_semaphore()

    def greet(step, carry):
        other = lax.rem(me + step, devices_all)
        pl.semaphore_signal(
            barrier, inc=1, device_id=(group, other // halves, lax.rem(other, halves)),
            device_id_type=MESH,
        )
        return carry

    lax.fori_loop(1, devices_all, greet, 0)

    small[0].wait()
    land = mask_ref[...].astype(F32)
    land_rows = [jnp.broadcast_to(land[r : r + 1], (angles, width)) for r in range(rows)]

    def row_of(j, r):
        return x_ref[j, pl.ds(r, angles, stride=rows), :] * land_rows[r]

    def stage(j, carry):
        down_out[j, pl.ds(0, angles), :] = row_of(j, rows - 1)
        second = row_of(j, rows - 2)
        down_out[j, pl.ds(angles, low), :] = second[:low]
        down_out[j, pl.ds(angles + low, low), :] = second[high:]
        up_out[j, pl.ds(0, angles), :] = row_of(j, 0)
        up_out[j, pl.ds(angles, side), :] = row_of(j, 1)[low:high]
        return carry

    def down_copy(g):
        part = pl.ds(starts[g], starts[g + 1] - starts[g])
        return pltpu.make_async_remote_copy(
            src_ref=down_out.at[part], dst_ref=down_in.at[part],
            send_sem=halo_send.at[0, g], recv_sem=halo_recv.at[0, g],
            device_id=(group, lax.rem(tile + 1, tiles), half), device_id_type=MESH,
        )

    def up_copy(g):
        part = pl.ds(starts[g], starts[g + 1] - starts[g])
        return pltpu.make_async_remote_copy(
            src_ref=up_out.at[part], dst_ref=up_in.at[part],
            send_sem=halo_send.at[1, g], recv_sem=halo_recv.at[1, g],
            device_id=(group, lax.rem(tile + tiles - 1, tiles), half), device_id_type=MESH,
        )

    for g in range(groups):
        load(g).wait()
        lax.fori_loop(starts[g], starts[g + 1], stage, 0)
        if g == 0:
            pl.semaphore_wait(barrier, devices_all - 1)

        @pl.when(tile < tiles - 1)
        def _():
            down_copy(g).start()

        @pl.when(tile > 0)
        def _():
            up_copy(g).start()

    @pl.when(tile == 0)
    def _():
        down_in[...] = jnp.zeros_like(down_in)

    @pl.when(tile == tiles - 1)
    def _():
        up_in[...] = jnp.zeros_like(up_in)

    for copy in small[1:]:
        copy.wait()
    far_up[...] = jnp.zeros_like(far_up)
    far_down[...] = jnp.zeros_like(far_down)
    aw_ref[...] = jnp.zeros_like(aw_ref)
    for r in range(rows):
        aw_ref[pl.ds(angles, 1), pl.ds(r * width, width)] = shift_ref[pl.ds(r, 1), :]
    cosines = trig_ref[0, :, :width]
    sines = trig_ref[1, :, :width]
    column = lax.broadcasted_iota(jnp.int32, (angles, width), 1)

    def tables(j, carry):
        index = (first + j).astype(F32)
        speed = courant_top * jnp.exp(jnp.full((1, width), -LOG_STEP, F32) * index)
        flux = stencil_weights(speed * cosines)
        for k, weight in enumerate(cell_weights(flux, flux)):
            wx_ref[j, k] = weight
        flux = stencil_weights(speed * sines)
        for k, weight in enumerate(cell_weights(flux, flux)):
            at = column + (k - 2)
            wy_ref[j, k] = jnp.where((at >= 0) & (at < width), weight, 0.0)
        return carry

    lax.fori_loop(0, local_f, tables, 0)

    wind_cos = jnp.cos(dir_ref[...]) * speed_ref[...]
    wind_sin = jnp.sin(dir_ref[...]) * speed_ref[...]
    for r in range(rows):
        turning = sines * gx_ref[pl.ds(r, 1), :] - cosines * gy_ref[pl.ds(r, 1), :]
        ring_ref[r, pl.ds(1, angles), :] = turning
        ring_ref[r, pl.ds(0, 1), :] = turning[angles - 1 :]
        ring_ref[r, pl.ds(angles + 1, 1), :] = turning[:1]
        lower = stencil_weights(0.5 * (ring_ref[r, pl.ds(0, angles), :] + turning))
        upper = stencil_weights(0.5 * (turning + ring_ref[r, pl.ds(2, angles), :]))
        for k, weight in enumerate(cell_weights(lower, upper)):
            wd_ref[r, k] = weight * land_rows[r]
        wind_ref[r] = cosines * wind_cos[r : r + 1] + sines * wind_sin[r : r + 1]

    slots = order_ref.shape[1]
    cells = rows * width
    at_cell = lax.broadcasted_iota(jnp.int32, (cells, slots), 0) == order_ref[...]
    at_cell = jnp.where(at_cell, 1.0, 0.0).astype(BF16)
    slot = lax.broadcasted_iota(jnp.int32, (devices_all * padded, slots), 1)
    line = lax.broadcasted_iota(jnp.int32, (devices_all * padded, slots), 0)
    shifted = slot.dtype.type(devices_all.bit_length() - 1)
    place = (slot & (devices_all - 1)) * padded + lax.shift_right_logical(
        slot, jnp.full(slot.shape, shifted, jnp.int32)
    )
    pick = jnp.where(line == place, 1.0, 0.0).astype(BF16)
    hot_ref[...] = lax.dot_general(
        pick, at_cell, (((1,), (1,)), ((), ())), preferred_element_type=F32
    ).astype(BF16)

    def advance(j, carry):
        a = [row_of(j, r) for r in range(rows)]
        up1 = down_in[j, pl.ds(0, angles), :]
        far_up[pl.ds(0, low), :] = down_in[j, pl.ds(angles, low), :]
        far_up[pl.ds(high, low), :] = down_in[j, pl.ds(angles + low, low), :]
        dn1 = up_in[j, pl.ds(0, angles), :]
        far_down[pl.ds(low, side), :] = up_in[j, pl.ds(angles, side), :]
        line_of = [far_up[...], up1, *a, dn1, far_down[...]]
        relative = jnp.exp(
            jnp.full((1, width), LOG_STEP, F32)
            * ((first + j).astype(F32) - 0.5 * (local_f * halves - 1))
        )
        for r in range(rows):
            ax = line_of[r] * wx_ref[j, 0]
            for k in range(1, 5):
                ax = ax + line_of[r + k] * wx_ref[j, k]
            ay = ax * wy_ref[j, 2]
            for k in (0, 1, 3, 4):
                ay = ay + pltpu.roll(ax, (2 - k) % width, 1) * wy_ref[j, k]
            ring_ref[r, pl.ds(2, angles), :] = ay
            ring_ref[r, pl.ds(0, 2), :] = ay[angles - 2 :]
            ring_ref[r, pl.ds(angles + 2, 2), :] = ay[:2]
            ar = ay * wd_ref[r, 2]
            for k in (0, 1, 3, 4):
                ar = ar + ring_ref[r, pl.ds(k, angles), :] * wd_ref[r, k]
            growth = 1.0 + wind_gain * jnp.maximum(wind_ref[r] * relative - 1.0, 0.0)
            aw_ref[pl.ds(pl.multiple_of(j * pitch, 8), angles), pl.ds(r * width, width)] = (
                ar * growth
            )
        return carry

    mine = pl.ds(pl.multiple_of(tile * padded, 8), padded)
    for g in range(groups):
        @pl.when(tile > 0)
        def _():
            down_copy(g).wait_recv()

        @pl.when(tile < tiles - 1)
        def _():
            up_copy(g).wait_recv()

        lax.fori_loop(starts[g], starts[g + 1], advance, 0)
        both = jnp.concatenate(two_parts(aw_ref[pl.ds(g * CHUNK, CHUNK), :]), axis=0)
        both = lax.dot_general(
            hot_ref[...], both, (((1,), (1,)), ((), ())), preferred_element_type=F32
        )
        send_ref[g] = both[:, :CHUNK] + both[:, CHUNK:]

        def send(step, carry):
            other = lax.rem(me + step, devices_all)
            theirs = pl.ds(pl.multiple_of(other * padded, 8), padded)
            pltpu.make_async_remote_copy(
                src_ref=send_ref.at[g, theirs], dst_ref=recv_ref.at[g, half, mine],
                send_sem=part_send.at[g], recv_sem=part_recv.at[g],
                device_id=(group, other // halves, lax.rem(other, halves)), device_id_type=MESH,
            ).start()
            return carry

        lax.fori_loop(1, devices_all, send, 0)
        own = pl.ds(pl.multiple_of(me * padded, 8), padded)
        pltpu.make_async_copy(
            send_ref.at[g, own], recv_ref.at[g, half, mine], part_recv.at[g]
        ).start()

    points = tiles * pair
    total_f = local_f * halves
    af_ref[pl.ds(0, 2 * pitch)] = jnp.zeros((2 * pitch, points), F32)
    af_ref[pl.ds((total_f + 2) * pitch, 2 * pitch)] = jnp.zeros((2 * pitch, points), F32)

    def relative_at(j, power):
        return jnp.exp(
            jnp.full((1, points), power * LOG_STEP, F32)
            * (j.astype(F32) - 0.5 * (total_f - 1))
        )

    def shift(j, carry):
        energy, inverse = carry
        base = pl.multiple_of(j * pitch, 8)
        af = af_ref[pl.ds(base, angles), :] * wf_ref[0]
        for k in range(1, 5):
            af = af + af_ref[pl.ds(base + k * pitch, angles), :] * wf_ref[k]
        out_ref[j] = af
        return energy + af, inverse + af * relative_at(j, -1.0)

    sums = (jnp.zeros((angles, points), F32), jnp.zeros((angles, points), F32))
    done = 0
    for g in range(groups):
        pltpu.make_async_copy(recv_ref.at[g], recv_ref.at[g], part_recv.at[g]).wait()
        height = min(CHUNK, local_f * pitch - g * CHUNK)
        for h in range(halves):
            turned = jnp.transpose(recv_ref[g, h])
            if padded != pair:
                line = lax.broadcasted_iota(jnp.int32, (tiles * padded, points), 0)
                slot = lax.broadcasted_iota(jnp.int32, (tiles * padded, points), 1)
                tile_of = lax.div(slot, jnp.full(slot.shape, pair, jnp.int32))
                keep = jnp.where(line == slot + tile_of * (padded - pair), 1.0, 0.0).astype(BF16)
                turned = sum(
                    jnp.dot(part, keep, preferred_element_type=F32) for part in two_parts(turned)
                )
            af_ref[pl.ds((2 + h * local_f) * pitch + g * CHUNK, height), :] = turned[:height]
        if g == 0:
            rate = af_ref[pl.ds(2 * pitch + angles, 1), :] * trig_ref[0, :, :points]
            flux = stencil_weights(rate)
            for k, weight in enumerate(cell_weights(flux, flux)):
                wf_ref[k] = weight
        if g < groups - 1:
            ready = max((g + 1) * CHUNK // pitch - 2, 0)
        else:
            ready = local_f
            for h in range(1, halves):
                sums = lax.fori_loop(h * local_f, h * local_f + 2, shift, sums)
        for h in range(halves):
            begin = max(done, 2) if h else done
            if ready > begin:
                sums = lax.fori_loop(h * local_f + begin, h * local_f + ready, shift, sums)
        done = max(done, ready)
    energy, inverse = sums
    scale = 1.0 / (total_f * angles)
    energy = jnp.sum(energy, axis=0, keepdims=True) * scale
    inverse = jnp.sum(inverse, axis=0, keepdims=True) * scale
    mean_freq = energy / jnp.maximum(inverse, reciprocal_lower_limit)
    square = mean_freq * mean_freq
    steep = energy * energy * (square * square * square * mean_freq) * (
        dissipation / steep_norm**2
    )

    steep_ref[...] = steep

    for g in range(groups):
        @pl.when(tile < tiles - 1)
        def _():
            down_copy(g).wait_send()

        @pl.when(tile > 0)
        def _():
            up_copy(g).wait_send()

        sent = send_ref.at[g, pl.ds(0, (devices_all - 1) * padded)]
        pltpu.make_async_copy(sent, sent, part_send.at[g]).wait()


def on_device(action, sea_mask, order, grad_x, grad_y, shift_rate, wind_speed, wind_dir):
    tiles = lax.axis_size("tile")
    halves = lax.axis_size("comp")
    local_f, angles, rows, width = action.shape
    total_f = local_f * halves
    devices_all = tiles * halves
    pair = order.shape[1] // devices_all
    padded = -(-pair // 8) * 8
    points = tiles * pair
    pitch = -(-angles // 8) * 8
    groups = -(-local_f * pitch // CHUNK)
    starts = tuple(min(-(-g * CHUNK // pitch), local_f) for g in range(groups)) + (local_f,)
    shape = (tiles, halves, local_f, angles, rows, width, pair, padded, pitch, starts)
    theta = (np.arange(angles) + 0.5) * (2.0 * np.pi / angles)
    trig = np.stack([np.cos(theta), np.sin(theta)]).astype(np.float32)
    trig = np.repeat(trig[:, :, None], max(points, width), axis=2)
    message = -(-(angles + angles // 2) // 8) * 8
    halo = pltpu.VMEM((local_f, message, width), F32)
    vmem = pl.BlockSpec(memory_space=pltpu.VMEM)
    shifted, steep = pl.pallas_call(
        functools.partial(kernel, shape),
        out_shape=(
            jax.ShapeDtypeStruct((total_f, angles, points), F32),
            jax.ShapeDtypeStruct((1, points), F32),
        ),
        in_specs=[pl.BlockSpec(memory_space=pltpu.HBM)] * 9,
        out_specs=(vmem, vmem),
        scratch_shapes=[
            pltpu.VMEM((local_f, angles * rows, width), F32),
            pltpu.VMEM((rows, width), jnp.int32),
            pltpu.VMEM(order.shape, jnp.int32),
            *[pltpu.VMEM((rows, width), F32)] * 5,
            pltpu.VMEM(trig.shape, F32),
            halo, halo, halo, halo,
            pltpu.VMEM((angles, width), F32),
            pltpu.VMEM((angles, width), F32),
            pltpu.VMEM((local_f, 5, angles, width), F32),
            pltpu.VMEM((local_f, 5, angles, width), F32),
            pltpu.VMEM((rows, 5, angles, width), F32),
            pltpu.VMEM((rows, angles, width), F32),
            pltpu.VMEM((rows, angles + 4, width), F32),
            pltpu.VMEM((groups * CHUNK, rows * width), F32),
            pltpu.VMEM((devices_all * padded, rows * width), BF16),
            pltpu.VMEM((groups, devices_all * padded, CHUNK), F32),
            pltpu.VMEM((groups, halves, tiles * padded, CHUNK), F32),
            pltpu.VMEM((5, angles, points), F32),
            pltpu.VMEM(((total_f + 4) * pitch, points), F32),
            pltpu.SemaphoreType.DMA((groups,)),
            pltpu.SemaphoreType.DMA((8,)),
            pltpu.SemaphoreType.DMA((2, groups)),
            pltpu.SemaphoreType.DMA((2, groups)),
            pltpu.SemaphoreType.DMA((groups,)),
            pltpu.SemaphoreType.DMA((groups,)),
        ],
        compiler_params=pltpu.CompilerParams(
            collective_id=0, has_side_effects=True, vmem_limit_bytes=63 * 1024 * 1024
        ),
    )(
        action.reshape(local_f, angles * rows, width), sea_mask, order, grad_x, grad_y,
        shift_rate, wind_speed, wind_dir, trig,
    )
    relative = np.float32(ratio_step) ** (np.arange(total_f, dtype=np.float32) - 0.5 * (total_f - 1))
    relative = jnp.asarray(relative.astype(np.float32))[:, None, None]
    return shifted / (1.0 + relative**2 * steep[None])


def solution(mesh):
    return jax.shard_map(
        on_device,
        mesh=mesh,
        in_specs=(
            P("comp", None, ("group", "tile"), None),
            P(("group", "tile"), None),
            P(("group", "tile"), None),
            P(("group", "tile"), None),
            P(("group", "tile"), None),
            P(("group", "tile"), None),
            P(("group", "tile"), None),
            P(("group", "tile"), None),
        ),
        out_specs=P(None, None, ("group", "tile", "comp")),
        check_vma=False,
    )
```

```python
import functools
import math

import jax
import jax.numpy as jnp
import numpy as np
from jax import lax
from jax.experimental import pallas as pl
from jax.experimental.pallas import tpu as pltpu
from jax.sharding import PartitionSpec as P

ratio_step = 1.07
courant_top = 0.8
wind_gain = 0.05
dissipation = 1.0
steep_norm = 0.1
reciprocal_lower_limit = 0.05
LOG_STEP = math.log(ratio_step)
CHUNK = 128
AHEAD = 2
MESH = pl.DeviceIdType.MESH
F32 = jnp.float32
BF16 = jnp.bfloat16


def stencil_weights(rate):
    k = (1.0 - rate * rate) * (1.0 / 6.0)
    kc = k * rate
    left = rate * (0.5 + 0.5 * rate)
    right = rate * (0.5 - 0.5 * rate)
    ahead = rate >= 0.0
    zero = jnp.zeros_like(rate)
    f0 = jnp.where(ahead, -kc, zero)
    f1 = left + jnp.where(ahead, 2.0 * kc, -kc)
    f2 = right + jnp.where(ahead, -kc, 2.0 * kc)
    f3 = jnp.where(ahead, zero, -kc)
    return f0, f1, f2, f3


def cell_weights(lower, upper):
    return (
        lower[0],
        lower[1] - upper[0],
        1.0 + lower[2] - upper[1],
        lower[3] - upper[2],
        -upper[3],
    )


def two_parts(value):
    high = value.astype(BF16)
    return high, (value - high.astype(F32)).astype(BF16)


def kernel(
    shape, x_hbm, mask_hbm, order_hbm, gx_hbm, gy_hbm, shift_hbm, speed_hbm, dir_hbm, trig_hbm,
    out_hbm, factor_ref,
    out_ref, x_ref, mask_ref, order_ref, gx_ref, gy_ref, shift_ref, speed_ref, dir_ref, trig_ref,
    down_out, up_out, down_in, up_in, far_up, far_down, wx_ref, wy_ref, wd_ref, wind_ref, ring_ref,
    aw_ref, hot_ref, send_ref, recv_ref, wf_ref, af_ref,
    out_sem, x_sem, small_sem, halo_send, halo_recv, part_send, part_recv,
):
    tiles, halves, local_f, angles, rows, width, pair, padded, pitch, starts = shape
    groups = len(starts) - 1
    devices_all = tiles * halves
    group, tile, half = lax.axis_index("group"), lax.axis_index("tile"), lax.axis_index("comp")
    me = tile * halves + half
    first = half * local_f
    low = angles // 4
    high = angles - low
    side = angles // 2

    small = [
        pltpu.make_async_copy(source, target, small_sem.at[i])
        for i, (source, target) in enumerate([
            (mask_hbm, mask_ref), (order_hbm, order_ref), (gx_hbm, gx_ref), (gy_hbm, gy_ref),
            (shift_hbm, shift_ref), (speed_hbm, speed_ref), (dir_hbm, dir_ref),
            (trig_hbm, trig_ref),
        ])
    ]

    def load(g):
        part = pl.ds(starts[g], starts[g + 1] - starts[g])
        return pltpu.make_async_copy(x_hbm.at[part], x_ref.at[part], x_sem.at[g])

    small[0].start()
    for g in range(groups):
        load(g).start()
    for copy in small[1:]:
        copy.start()

    barrier = pltpu.get_barrier_semaphore()

    def greet(step, carry):
        other = lax.rem(me + step, devices_all)
        pl.semaphore_signal(
            barrier, inc=1, device_id=(group, other // halves, lax.rem(other, halves)),
            device_id_type=MESH,
        )
        return carry

    lax.fori_loop(1, devices_all, greet, 0)

    small[0].wait()
    land = mask_ref[...].astype(F32)
    land_rows = [jnp.broadcast_to(land[r : r + 1], (angles, width)) for r in range(rows)]

    def row_of(j, r):
        return x_ref[j, pl.ds(r, angles, stride=rows), :] * land_rows[r]

    def stage(j, carry):
        down_out[j, pl.ds(0, angles), :] = row_of(j, rows - 1)
        second = row_of(j, rows - 2)
        down_out[j, pl.ds(angles, low), :] = second[:low]
        down_out[j, pl.ds(angles + low, low), :] = second[high:]
        up_out[j, pl.ds(0, angles), :] = row_of(j, 0)
        up_out[j, pl.ds(angles, side), :] = row_of(j, 1)[low:high]
        return carry

    def down_copy(g):
        part = pl.ds(starts[g], starts[g + 1] - starts[g])
        return pltpu.make_async_remote_copy(
            src_ref=down_out.at[part], dst_ref=down_in.at[part],
            send_sem=halo_send.at[0, g], recv_sem=halo_recv.at[0, g],
            device_id=(group, lax.rem(tile + 1, tiles), half), device_id_type=MESH,
        )

    def up_copy(g):
        part = pl.ds(starts[g], starts[g + 1] - starts[g])
        return pltpu.make_async_remote_copy(
            src_ref=up_out.at[part], dst_ref=up_in.at[part],
            send_sem=halo_send.at[1, g], recv_sem=halo_recv.at[1, g],
            device_id=(group, lax.rem(tile + tiles - 1, tiles), half), device_id_type=MESH,
        )

    def start_halo(g):
        @pl.when(tile < tiles - 1)
        def _():
            down_copy(g).start()

        @pl.when(tile > 0)
        def _():
            up_copy(g).start()

    for g in range(groups):
        load(g).wait()
        lax.fori_loop(starts[g], starts[g + 1], stage, 0)
        if g == 0:
            pl.semaphore_wait(barrier, devices_all - 1)
        if g < AHEAD:
            start_halo(g)

    @pl.when(tile == 0)
    def _():
        down_in[...] = jnp.zeros_like(down_in)

    @pl.when(tile == tiles - 1)
    def _():
        up_in[...] = jnp.zeros_like(up_in)

    for copy in small[1:]:
        copy.wait()
    far_up[...] = jnp.zeros_like(far_up)
    far_down[...] = jnp.zeros_like(far_down)
    aw_ref[...] = jnp.zeros_like(aw_ref)
    for r in range(rows):
        aw_ref[pl.ds(angles, 1), pl.ds(r * width, width)] = shift_ref[pl.ds(r, 1), :]
    cosines = trig_ref[0, :, :width]
    sines = trig_ref[1, :, :width]
    column = lax.broadcasted_iota(jnp.int32, (angles, width), 1)

    def tables(j, carry):
        index = (first + j).astype(F32)
        speed = courant_top * jnp.exp(jnp.full((1, width), -LOG_STEP, F32) * index)
        flux = stencil_weights(speed * cosines)
        for k, weight in enumerate(cell_weights(flux, flux)):
            wx_ref[j, k] = weight
        flux = stencil_weights(speed * sines)
        for k, weight in enumerate(cell_weights(flux, flux)):
            at = column + (k - 2)
            wy_ref[j, k] = jnp.where((at >= 0) & (at < width), weight, 0.0)
        return carry

    lax.fori_loop(0, local_f, tables, 0)

    wind_cos = jnp.cos(dir_ref[...]) * speed_ref[...]
    wind_sin = jnp.sin(dir_ref[...]) * speed_ref[...]
    for r in range(rows):
        turning = sines * gx_ref[pl.ds(r, 1), :] - cosines * gy_ref[pl.ds(r, 1), :]
        ring_ref[r, pl.ds(1, angles), :] = turning
        ring_ref[r, pl.ds(0, 1), :] = turning[angles - 1 :]
        ring_ref[r, pl.ds(angles + 1, 1), :] = turning[:1]
        lower = stencil_weights(0.5 * (ring_ref[r, pl.ds(0, angles), :] + turning))
        upper = stencil_weights(0.5 * (turning + ring_ref[r, pl.ds(2, angles), :]))
        for k, weight in enumerate(cell_weights(lower, upper)):
            wd_ref[r, k] = weight * land_rows[r]
        wind_ref[r] = cosines * wind_cos[r : r + 1] + sines * wind_sin[r : r + 1]

    slots = order_ref.shape[1]
    cells = rows * width
    at_cell = lax.broadcasted_iota(jnp.int32, (cells, slots), 0) == order_ref[...]
    at_cell = jnp.where(at_cell, 1.0, 0.0).astype(BF16)
    slot = lax.broadcasted_iota(jnp.int32, (devices_all * padded, slots), 1)
    line = lax.broadcasted_iota(jnp.int32, (devices_all * padded, slots), 0)
    shifted = slot.dtype.type(devices_all.bit_length() - 1)
    place = (slot & (devices_all - 1)) * padded + lax.shift_right_logical(
        slot, jnp.full(slot.shape, shifted, jnp.int32)
    )
    pick = jnp.where(line == place, 1.0, 0.0).astype(BF16)
    hot_ref[...] = lax.dot_general(
        pick, at_cell, (((1,), (1,)), ((), ())), preferred_element_type=F32
    ).astype(BF16)

    def advance(j, carry):
        a = [row_of(j, r) for r in range(rows)]
        up1 = down_in[j, pl.ds(0, angles), :]
        far_up[pl.ds(0, low), :] = down_in[j, pl.ds(angles, low), :]
        far_up[pl.ds(high, low), :] = down_in[j, pl.ds(angles + low, low), :]
        dn1 = up_in[j, pl.ds(0, angles), :]
        far_down[pl.ds(low, side), :] = up_in[j, pl.ds(angles, side), :]
        line_of = [far_up[...], up1, *a, dn1, far_down[...]]
        relative = jnp.exp(
            jnp.full((1, width), LOG_STEP, F32)
            * ((first + j).astype(F32) - 0.5 * (local_f * halves - 1))
        )
        for r in range(rows):
            ax = line_of[r] * wx_ref[j, 0]
            for k in range(1, 5):
                ax = ax + line_of[r + k] * wx_ref[j, k]
            ay = ax * wy_ref[j, 2]
            for k in (0, 1, 3, 4):
                ay = ay + pltpu.roll(ax, (2 - k) % width, 1) * wy_ref[j, k]
            ring_ref[r, pl.ds(2, angles), :] = ay
            ring_ref[r, pl.ds(0, 2), :] = ay[angles - 2 :]
            ring_ref[r, pl.ds(angles + 2, 2), :] = ay[:2]
            ar = ay * wd_ref[r, 2]
            for k in (0, 1, 3, 4):
                ar = ar + ring_ref[r, pl.ds(k, angles), :] * wd_ref[r, k]
            growth = 1.0 + wind_gain * jnp.maximum(wind_ref[r] * relative - 1.0, 0.0)
            aw_ref[pl.ds(pl.multiple_of(j * pitch, 8), angles), pl.ds(r * width, width)] = (
                ar * growth
            )
        return carry

    mine = pl.ds(pl.multiple_of(tile * padded, 8), padded)
    for g in range(groups):
        @pl.when(tile > 0)
        def _():
            down_copy(g).wait_recv()

        @pl.when(tile < tiles - 1)
        def _():
            up_copy(g).wait_recv()

        if g + AHEAD < groups:
            start_halo(g + AHEAD)
        lax.fori_loop(starts[g], starts[g + 1], advance, 0)
        both = jnp.concatenate(two_parts(aw_ref[pl.ds(g * CHUNK, CHUNK), :]), axis=0)
        both = lax.dot_general(
            hot_ref[...], both, (((1,), (1,)), ((), ())), preferred_element_type=F32
        )
        send_ref[g] = both[:, :CHUNK] + both[:, CHUNK:]

        def send(step, carry):
            other = lax.rem(me + step, devices_all)
            theirs = pl.ds(pl.multiple_of(other * padded, 8), padded)
            pltpu.make_async_remote_copy(
                src_ref=send_ref.at[g, theirs], dst_ref=recv_ref.at[g, half, mine],
                send_sem=part_send.at[g], recv_sem=part_recv.at[g],
                device_id=(group, other // halves, lax.rem(other, halves)), device_id_type=MESH,
            ).start()
            return carry

        lax.fori_loop(1, devices_all, send, 0)
        own = pl.ds(pl.multiple_of(me * padded, 8), padded)
        pltpu.make_async_copy(
            send_ref.at[g, own], recv_ref.at[g, half, mine], part_recv.at[g]
        ).start()

    points = tiles * pair
    total_f = local_f * halves
    af_ref[pl.ds(0, 2 * pitch)] = jnp.zeros((2 * pitch, points), F32)
    af_ref[pl.ds((total_f + 2) * pitch, 2 * pitch)] = jnp.zeros((2 * pitch, points), F32)

    def relative_at(j, power):
        return jnp.exp(
            jnp.full((1, points), power * LOG_STEP, F32)
            * (j.astype(F32) - 0.5 * (total_f - 1))
        )

    def shift(j, carry):
        energy, inverse = carry
        base = pl.multiple_of(j * pitch, 8)
        af = af_ref[pl.ds(base, angles), :] * wf_ref[0]
        for k in range(1, 5):
            af = af + af_ref[pl.ds(base + k * pitch, angles), :] * wf_ref[k]
        out_ref[j] = af
        return energy + af, inverse + af * relative_at(j, -1.0)

    sums = (jnp.zeros((angles, points), F32), jnp.zeros((angles, points), F32))
    done = 0
    leaving = []

    def shift_range(begin, end, sums):
        sums = lax.fori_loop(begin, end, shift, sums)
        part = pl.ds(begin, end - begin)
        leaving.append(
            pltpu.make_async_copy(out_ref.at[part], out_hbm.at[part], out_sem.at[len(leaving)])
        )
        leaving[-1].start()
        return sums

    for g in range(groups):
        pltpu.make_async_copy(recv_ref.at[g], recv_ref.at[g], part_recv.at[g]).wait()
        height = min(CHUNK, local_f * pitch - g * CHUNK)
        for h in range(halves):
            turned = jnp.transpose(recv_ref[g, h])
            if padded != pair:
                line = lax.broadcasted_iota(jnp.int32, (tiles * padded, points), 0)
                slot = lax.broadcasted_iota(jnp.int32, (tiles * padded, points), 1)
                tile_of = lax.div(slot, jnp.full(slot.shape, pair, jnp.int32))
                keep = jnp.where(line == slot + tile_of * (padded - pair), 1.0, 0.0).astype(BF16)
                turned = sum(
                    jnp.dot(part, keep, preferred_element_type=F32) for part in two_parts(turned)
                )
            af_ref[pl.ds((2 + h * local_f) * pitch + g * CHUNK, height), :] = turned[:height]
        if g == 0:
            rate = af_ref[pl.ds(2 * pitch + angles, 1), :] * trig_ref[0, :, :points]
            flux = stencil_weights(rate)
            for k, weight in enumerate(cell_weights(flux, flux)):
                wf_ref[k] = weight
        if g < groups - 1:
            ready = max((g + 1) * CHUNK // pitch - 2, 0)
        else:
            ready = local_f
            for h in range(1, halves):
                sums = shift_range(h * local_f, h * local_f + 2, sums)
        for h in range(halves):
            begin = max(done, 2) if h else done
            if ready > begin:
                sums = shift_range(h * local_f + begin, h * local_f + ready, sums)
        done = max(done, ready)
    energy, inverse = sums
    scale = 1.0 / (total_f * angles)
    energy = jnp.sum(energy, axis=0, keepdims=True) * scale
    inverse = jnp.sum(inverse, axis=0, keepdims=True) * scale
    mean_freq = energy / jnp.maximum(inverse, reciprocal_lower_limit)
    square = mean_freq * mean_freq
    steep = energy * energy * (square * square * square * mean_freq) * (
        dissipation / steep_norm**2
    )

    index = lax.broadcasted_iota(jnp.int32, (total_f, 1, points), 0).astype(F32)
    relative = jnp.exp(LOG_STEP * (index - 0.5 * (total_f - 1)))
    factor_ref[...] = 1.0 / (1.0 + relative * relative * steep[None])

    for copy in leaving:
        copy.wait()
    for g in range(groups):
        @pl.when(tile < tiles - 1)
        def _():
            down_copy(g).wait_send()

        @pl.when(tile > 0)
        def _():
            up_copy(g).wait_send()

        sent = send_ref.at[g, pl.ds(0, (devices_all - 1) * padded)]
        pltpu.make_async_copy(sent, sent, part_send.at[g]).wait()


def on_device(action, sea_mask, order, grad_x, grad_y, shift_rate, wind_speed, wind_dir):
    tiles = lax.axis_size("tile")
    halves = lax.axis_size("comp")
    local_f, angles, rows, width = action.shape
    total_f = local_f * halves
    devices_all = tiles * halves
    pair = order.shape[1] // devices_all
    padded = -(-pair // 8) * 8
    points = tiles * pair
    pitch = -(-angles // 8) * 8
    groups = -(-local_f * pitch // CHUNK)
    starts = tuple(min(-(-g * CHUNK // pitch), local_f) for g in range(groups)) + (local_f,)
    shape = (tiles, halves, local_f, angles, rows, width, pair, padded, pitch, starts)
    theta = (np.arange(angles) + 0.5) * (2.0 * np.pi / angles)
    trig = np.stack([np.cos(theta), np.sin(theta)]).astype(np.float32)
    trig = np.repeat(trig[:, :, None], max(points, width), axis=2)
    message = -(-(angles + angles // 2) // 8) * 8
    halo = pltpu.VMEM((local_f, message, width), F32)
    vmem = pl.BlockSpec(memory_space=pltpu.VMEM)
    shifted, factor = pl.pallas_call(
        functools.partial(kernel, shape),
        out_shape=(
            jax.ShapeDtypeStruct((total_f, angles, points), F32),
            jax.ShapeDtypeStruct((total_f, 1, points), F32),
        ),
        in_specs=[pl.BlockSpec(memory_space=pltpu.HBM)] * 9,
        out_specs=(pl.BlockSpec(memory_space=pltpu.HBM), vmem),
        scratch_shapes=[
            pltpu.VMEM((total_f, angles, points), F32),
            pltpu.VMEM((local_f, angles * rows, width), F32),
            pltpu.VMEM((rows, width), jnp.int32),
            pltpu.VMEM(order.shape, jnp.int32),
            *[pltpu.VMEM((rows, width), F32)] * 5,
            pltpu.VMEM(trig.shape, F32),
            halo, halo, halo, halo,
            pltpu.VMEM((angles, width), F32),
            pltpu.VMEM((angles, width), F32),
            pltpu.VMEM((local_f, 5, angles, width), F32),
            pltpu.VMEM((local_f, 5, angles, width), F32),
            pltpu.VMEM((rows, 5, angles, width), F32),
            pltpu.VMEM((rows, angles, width), F32),
            pltpu.VMEM((rows, angles + 4, width), F32),
            pltpu.VMEM((groups * CHUNK, rows * width), F32),
            pltpu.VMEM((devices_all * padded, rows * width), BF16),
            pltpu.VMEM((groups, devices_all * padded, CHUNK), F32),
            pltpu.VMEM((groups, halves, tiles * padded, CHUNK), F32),
            pltpu.VMEM((5, angles, points), F32),
            pltpu.VMEM(((total_f + 4) * pitch, points), F32),
            pltpu.SemaphoreType.DMA(((groups + 1) * halves,)),
            pltpu.SemaphoreType.DMA((groups,)),
            pltpu.SemaphoreType.DMA((8,)),
            pltpu.SemaphoreType.DMA((2, groups)),
            pltpu.SemaphoreType.DMA((2, groups)),
            pltpu.SemaphoreType.DMA((groups,)),
            pltpu.SemaphoreType.DMA((groups,)),
        ],
        compiler_params=pltpu.CompilerParams(
            collective_id=0, has_side_effects=True, vmem_limit_bytes=63 * 1024 * 1024
        ),
    )(
        action.reshape(local_f, angles * rows, width), sea_mask, order, grad_x, grad_y,
        shift_rate, wind_speed, wind_dir, trig,
    )
    return shifted * factor


def solution(mesh):
    return jax.shard_map(
        on_device,
        mesh=mesh,
        in_specs=(
            P("comp", None, ("group", "tile"), None),
            P(("group", "tile"), None),
            P(("group", "tile"), None),
            P(("group", "tile"), None),
            P(("group", "tile"), None),
            P(("group", "tile"), None),
            P(("group", "tile"), None),
            P(("group", "tile"), None),
        ),
        out_specs=P(None, None, ("group", "tile", "comp")),
        check_vma=False,
    )
```

```python
import functools
import math

import jax
import jax.numpy as jnp
import numpy as np
from jax import lax
from jax.experimental import pallas as pl
from jax.experimental.pallas import tpu as pltpu
from jax.sharding import PartitionSpec as P

ratio_step = 1.07
courant_top = 0.8
wind_gain = 0.05
dissipation = 1.0
steep_norm = 0.1
reciprocal_lower_limit = 0.05
LOG_STEP = math.log(ratio_step)
CHUNK = 128
AHEAD = 2
MESH = pl.DeviceIdType.MESH
F32 = jnp.float32
BF16 = jnp.bfloat16


def stencil_weights(rate):
    k = (1.0 - rate * rate) * (1.0 / 6.0)
    kc = k * rate
    left = rate * (0.5 + 0.5 * rate)
    right = rate * (0.5 - 0.5 * rate)
    ahead = rate >= 0.0
    zero = jnp.zeros_like(rate)
    f0 = jnp.where(ahead, -kc, zero)
    f1 = left + jnp.where(ahead, 2.0 * kc, -kc)
    f2 = right + jnp.where(ahead, -kc, 2.0 * kc)
    f3 = jnp.where(ahead, zero, -kc)
    return f0, f1, f2, f3


def cell_weights(lower, upper):
    return (
        lower[0],
        lower[1] - upper[0],
        1.0 + lower[2] - upper[1],
        lower[3] - upper[2],
        -upper[3],
    )


def two_parts(value):
    high = value.astype(BF16)
    return high, (value - high.astype(F32)).astype(BF16)


def kernel(
    shape, x_hbm, mask_hbm, order_hbm, gx_hbm, gy_hbm, shift_hbm, speed_hbm, dir_hbm, trig_hbm,
    out_hbm, factor_ref,
    out_ref, x_ref, mask_ref, order_ref, gx_ref, gy_ref, shift_ref, speed_ref, dir_ref, trig_ref,
    down_out, up_out, down_in, up_in, far_up, far_down, wx_ref, wy_ref, wd_ref, wind_ref, ring_ref,
    aw_ref, hot_ref, send_ref, recv_ref, wf_ref, af_ref,
    out_sem, x_sem, small_sem, halo_send, halo_recv, part_send, part_recv,
):
    tiles, halves, local_f, angles, rows, width, pair, padded, pitch, starts = shape
    groups = len(starts) - 1
    devices_all = tiles * halves
    group, tile, half = lax.axis_index("group"), lax.axis_index("tile"), lax.axis_index("comp")
    me = tile * halves + half
    first = half * local_f
    low = angles // 4
    high = angles - low
    side = angles // 2

    small = [
        pltpu.make_async_copy(source, target, small_sem.at[i])
        for i, (source, target) in enumerate([
            (mask_hbm, mask_ref), (order_hbm, order_ref), (gx_hbm, gx_ref), (gy_hbm, gy_ref),
            (shift_hbm, shift_ref), (speed_hbm, speed_ref), (dir_hbm, dir_ref),
            (trig_hbm, trig_ref),
        ])
    ]

    def load(g):
        part = pl.ds(starts[g], starts[g + 1] - starts[g])
        return pltpu.make_async_copy(x_hbm.at[part], x_ref.at[part], x_sem.at[g])

    small[0].start()
    for g in range(groups):
        load(g).start()
    for copy in small[1:]:
        copy.start()

    barrier = pltpu.get_barrier_semaphore()

    def greet(step, carry):
        other = lax.rem(me + step, devices_all)
        pl.semaphore_signal(
            barrier, inc=1, device_id=(group, other // halves, lax.rem(other, halves)),
            device_id_type=MESH,
        )
        return carry

    lax.fori_loop(1, devices_all, greet, 0)

    small[0].wait()
    land = mask_ref[...].astype(F32)
    land_rows = [jnp.broadcast_to(land[r : r + 1], (angles, width)) for r in range(rows)]

    def row_of(j, r):
        return x_ref[j, pl.ds(r, angles, stride=rows), :] * land_rows[r]

    def stage(j, carry):
        down_out[j, pl.ds(0, angles), :] = row_of(j, rows - 1)
        second = row_of(j, rows - 2)
        down_out[j, pl.ds(angles, low), :] = second[:low]
        down_out[j, pl.ds(angles + low, low), :] = second[high:]
        up_out[j, pl.ds(0, angles), :] = row_of(j, 0)
        up_out[j, pl.ds(angles, side), :] = row_of(j, 1)[low:high]
        return carry

    def down_copy(g):
        part = pl.ds(starts[g], starts[g + 1] - starts[g])
        return pltpu.make_async_remote_copy(
            src_ref=down_out.at[part], dst_ref=down_in.at[part],
            send_sem=halo_send.at[0, g], recv_sem=halo_recv.at[0, g],
            device_id=(group, lax.rem(tile + 1, tiles), half), device_id_type=MESH,
        )

    def up_copy(g):
        part = pl.ds(starts[g], starts[g + 1] - starts[g])
        return pltpu.make_async_remote_copy(
            src_ref=up_out.at[part], dst_ref=up_in.at[part],
            send_sem=halo_send.at[1, g], recv_sem=halo_recv.at[1, g],
            device_id=(group, lax.rem(tile + tiles - 1, tiles), half), device_id_type=MESH,
        )

    for copy in small[1:]:
        copy.wait()
    far_up[...] = jnp.zeros_like(far_up)
    far_down[...] = jnp.zeros_like(far_down)
    aw_ref[...] = jnp.zeros_like(aw_ref)
    for r in range(rows):
        aw_ref[pl.ds(angles, 1), pl.ds(r * width, width)] = shift_ref[pl.ds(r, 1), :]
    cosines = trig_ref[0, :, :width]
    sines = trig_ref[1, :, :width]
    column = lax.broadcasted_iota(jnp.int32, (angles, width), 1)

    def tables(j, carry):
        index = (first + j).astype(F32)
        speed = courant_top * jnp.exp(jnp.full((1, width), -LOG_STEP, F32) * index)
        flux = stencil_weights(speed * cosines)
        for k, weight in enumerate(cell_weights(flux, flux)):
            wx_ref[j, k] = weight
        flux = stencil_weights(speed * sines)
        for k, weight in enumerate(cell_weights(flux, flux)):
            at = column + (k - 2)
            wy_ref[j, k] = jnp.where((at >= 0) & (at < width), weight, 0.0)
        return carry

    lax.fori_loop(0, local_f, tables, 0)

    wind_cos = jnp.cos(dir_ref[...]) * speed_ref[...]
    wind_sin = jnp.sin(dir_ref[...]) * speed_ref[...]
    for r in range(rows):
        turning = sines * gx_ref[pl.ds(r, 1), :] - cosines * gy_ref[pl.ds(r, 1), :]
        ring_ref[r, pl.ds(1, angles), :] = turning
        ring_ref[r, pl.ds(0, 1), :] = turning[angles - 1 :]
        ring_ref[r, pl.ds(angles + 1, 1), :] = turning[:1]
        lower = stencil_weights(0.5 * (ring_ref[r, pl.ds(0, angles), :] + turning))
        upper = stencil_weights(0.5 * (turning + ring_ref[r, pl.ds(2, angles), :]))
        for k, weight in enumerate(cell_weights(lower, upper)):
            wd_ref[r, k] = weight * land_rows[r]
        wind_ref[r] = cosines * wind_cos[r : r + 1] + sines * wind_sin[r : r + 1]

    slots = order_ref.shape[1]
    cells = rows * width
    at_cell = lax.broadcasted_iota(jnp.int32, (cells, slots), 0) == order_ref[...]
    at_cell = jnp.where(at_cell, 1.0, 0.0).astype(BF16)
    slot = lax.broadcasted_iota(jnp.int32, (devices_all * padded, slots), 1)
    line = lax.broadcasted_iota(jnp.int32, (devices_all * padded, slots), 0)
    shifted = slot.dtype.type(devices_all.bit_length() - 1)
    place = (slot & (devices_all - 1)) * padded + lax.shift_right_logical(
        slot, jnp.full(slot.shape, shifted, jnp.int32)
    )
    pick = jnp.where(line == place, 1.0, 0.0).astype(BF16)
    hot_ref[...] = lax.dot_general(
        pick, at_cell, (((1,), (1,)), ((), ())), preferred_element_type=F32
    ).astype(BF16)

    def start_halo(g):
        @pl.when(tile < tiles - 1)
        def _():
            down_copy(g).start()

        @pl.when(tile > 0)
        def _():
            up_copy(g).start()

    for g in range(groups):
        load(g).wait()
        lax.fori_loop(starts[g], starts[g + 1], stage, 0)
        if g == 0:
            pl.semaphore_wait(barrier, devices_all - 1)
        if g < AHEAD:
            start_halo(g)

    @pl.when(tile == 0)
    def _():
        down_in[...] = jnp.zeros_like(down_in)

    @pl.when(tile == tiles - 1)
    def _():
        up_in[...] = jnp.zeros_like(up_in)

    def advance(j, carry):
        a = [row_of(j, r) for r in range(rows)]
        up1 = down_in[j, pl.ds(0, angles), :]
        far_up[pl.ds(0, low), :] = down_in[j, pl.ds(angles, low), :]
        far_up[pl.ds(high, low), :] = down_in[j, pl.ds(angles + low, low), :]
        dn1 = up_in[j, pl.ds(0, angles), :]
        far_down[pl.ds(low, side), :] = up_in[j, pl.ds(angles, side), :]
        line_of = [far_up[...], up1, *a, dn1, far_down[...]]
        relative = jnp.exp(
            jnp.full((1, width), LOG_STEP, F32)
            * ((first + j).astype(F32) - 0.5 * (local_f * halves - 1))
        )
        for r in range(rows):
            ax = line_of[r] * wx_ref[j, 0]
            for k in range(1, 5):
                ax = ax + line_of[r + k] * wx_ref[j, k]
            ay = ax * wy_ref[j, 2]
            for k in (0, 1, 3, 4):
                ay = ay + pltpu.roll(ax, (2 - k) % width, 1) * wy_ref[j, k]
            ring_ref[r, pl.ds(2, angles), :] = ay
            ring_ref[r, pl.ds(0, 2), :] = ay[angles - 2 :]
            ring_ref[r, pl.ds(angles + 2, 2), :] = ay[:2]
            ar = ay * wd_ref[r, 2]
            for k in (0, 1, 3, 4):
                ar = ar + ring_ref[r, pl.ds(k, angles), :] * wd_ref[r, k]
            growth = 1.0 + wind_gain * jnp.maximum(wind_ref[r] * relative - 1.0, 0.0)
            aw_ref[pl.ds(pl.multiple_of(j * pitch, 8), angles), pl.ds(r * width, width)] = (
                ar * growth
            )
        return carry

    mine = pl.ds(pl.multiple_of(tile * padded, 8), padded)
    for g in range(groups):
        @pl.when(tile > 0)
        def _():
            down_copy(g).wait_recv()

        @pl.when(tile < tiles - 1)
        def _():
            up_copy(g).wait_recv()

        if g + AHEAD < groups:
            start_halo(g + AHEAD)
        lax.fori_loop(starts[g], starts[g + 1], advance, 0)
        both = jnp.concatenate(two_parts(aw_ref[pl.ds(g * CHUNK, CHUNK), :]), axis=0)
        both = lax.dot_general(
            hot_ref[...], both, (((1,), (1,)), ((), ())), preferred_element_type=F32
        )
        send_ref[g] = both[:, :CHUNK] + both[:, CHUNK:]

        def send(step, carry):
            other = lax.rem(me + step, devices_all)
            theirs = pl.ds(pl.multiple_of(other * padded, 8), padded)
            pltpu.make_async_remote_copy(
                src_ref=send_ref.at[g, theirs], dst_ref=recv_ref.at[g, half, mine],
                send_sem=part_send.at[g], recv_sem=part_recv.at[g],
                device_id=(group, other // halves, lax.rem(other, halves)), device_id_type=MESH,
            ).start()
            return carry

        lax.fori_loop(1, devices_all, send, 0)
        own = pl.ds(pl.multiple_of(me * padded, 8), padded)
        pltpu.make_async_copy(
            send_ref.at[g, own], recv_ref.at[g, half, mine], part_recv.at[g]
        ).start()

    points = tiles * pair
    total_f = local_f * halves
    af_ref[pl.ds(0, 2 * pitch)] = jnp.zeros((2 * pitch, points), F32)
    af_ref[pl.ds((total_f + 2) * pitch, 2 * pitch)] = jnp.zeros((2 * pitch, points), F32)

    def relative_at(j, power):
        return jnp.exp(
            jnp.full((1, points), power * LOG_STEP, F32)
            * (j.astype(F32) - 0.5 * (total_f - 1))
        )

    def shift(j, carry):
        energy, inverse = carry
        base = pl.multiple_of(j * pitch, 8)
        af = af_ref[pl.ds(base, angles), :] * wf_ref[0]
        for k in range(1, 5):
            af = af + af_ref[pl.ds(base + k * pitch, angles), :] * wf_ref[k]
        out_ref[j] = af
        return energy + af, inverse + af * relative_at(j, -1.0)

    sums = (jnp.zeros((angles, points), F32), jnp.zeros((angles, points), F32))
    done = 0
    leaving = []

    def shift_range(begin, end, sums):
        sums = lax.fori_loop(begin, end, shift, sums)
        part = pl.ds(begin, end - begin)
        leaving.append(
            pltpu.make_async_copy(out_ref.at[part], out_hbm.at[part], out_sem.at[len(leaving)])
        )
        leaving[-1].start()
        return sums

    for g in range(groups):
        pltpu.make_async_copy(recv_ref.at[g], recv_ref.at[g], part_recv.at[g]).wait()
        height = min(CHUNK, local_f * pitch - g * CHUNK)
        for h in range(halves):
            turned = jnp.transpose(recv_ref[g, h])
            if padded != pair:
                line = lax.broadcasted_iota(jnp.int32, (tiles * padded, points), 0)
                slot = lax.broadcasted_iota(jnp.int32, (tiles * padded, points), 1)
                tile_of = lax.div(slot, jnp.full(slot.shape, pair, jnp.int32))
                keep = jnp.where(line == slot + tile_of * (padded - pair), 1.0, 0.0).astype(BF16)
                turned = sum(
                    jnp.dot(part, keep, preferred_element_type=F32) for part in two_parts(turned)
                )
            af_ref[pl.ds((2 + h * local_f) * pitch + g * CHUNK, height), :] = turned[:height]
        if g == 0:
            rate = af_ref[pl.ds(2 * pitch + angles, 1), :] * trig_ref[0, :, :points]
            flux = stencil_weights(rate)
            for k, weight in enumerate(cell_weights(flux, flux)):
                wf_ref[k] = weight
        if g < groups - 1:
            ready = max((g + 1) * CHUNK // pitch - 2, 0)
        else:
            ready = local_f
            for h in range(1, halves):
                sums = shift_range(h * local_f, h * local_f + 2, sums)
        for h in range(halves):
            begin = max(done, 2) if h else done
            if ready > begin:
                sums = shift_range(h * local_f + begin, h * local_f + ready, sums)
        done = max(done, ready)
    energy, inverse = sums
    scale = 1.0 / (total_f * angles)
    energy = jnp.sum(energy, axis=0, keepdims=True) * scale
    inverse = jnp.sum(inverse, axis=0, keepdims=True) * scale
    mean_freq = energy / jnp.maximum(inverse, reciprocal_lower_limit)
    square = mean_freq * mean_freq
    steep = energy * energy * (square * square * square * mean_freq) * (
        dissipation / steep_norm**2
    )

    index = lax.broadcasted_iota(jnp.int32, (total_f, 1, points), 0).astype(F32)
    relative = jnp.exp(LOG_STEP * (index - 0.5 * (total_f - 1)))
    factor_ref[...] = 1.0 / (1.0 + relative * relative * steep[None])

    for copy in leaving:
        copy.wait()
    for g in range(groups):
        @pl.when(tile < tiles - 1)
        def _():
            down_copy(g).wait_send()

        @pl.when(tile > 0)
        def _():
            up_copy(g).wait_send()

        sent = send_ref.at[g, pl.ds(0, (devices_all - 1) * padded)]
        pltpu.make_async_copy(sent, sent, part_send.at[g]).wait()


def on_device(action, sea_mask, order, grad_x, grad_y, shift_rate, wind_speed, wind_dir):
    tiles = lax.axis_size("tile")
    halves = lax.axis_size("comp")
    local_f, angles, rows, width = action.shape
    total_f = local_f * halves
    devices_all = tiles * halves
    pair = order.shape[1] // devices_all
    padded = -(-pair // 8) * 8
    points = tiles * pair
    pitch = -(-angles // 8) * 8
    groups = -(-local_f * pitch // CHUNK)
    starts = tuple(min(-(-g * CHUNK // pitch), local_f) for g in range(groups)) + (local_f,)
    shape = (tiles, halves, local_f, angles, rows, width, pair, padded, pitch, starts)
    theta = (np.arange(angles) + 0.5) * (2.0 * np.pi / angles)
    trig = np.stack([np.cos(theta), np.sin(theta)]).astype(np.float32)
    trig = np.repeat(trig[:, :, None], max(points, width), axis=2)
    message = -(-(angles + angles // 2) // 8) * 8
    halo = pltpu.VMEM((local_f, message, width), F32)
    vmem = pl.BlockSpec(memory_space=pltpu.VMEM)
    shifted, factor = pl.pallas_call(
        functools.partial(kernel, shape),
        out_shape=(
            jax.ShapeDtypeStruct((total_f, angles, points), F32),
            jax.ShapeDtypeStruct((total_f, 1, points), F32),
        ),
        in_specs=[pl.BlockSpec(memory_space=pltpu.HBM)] * 9,
        out_specs=(pl.BlockSpec(memory_space=pltpu.HBM), vmem),
        scratch_shapes=[
            pltpu.VMEM((total_f, angles, points), F32),
            pltpu.VMEM((local_f, angles * rows, width), F32),
            pltpu.VMEM((rows, width), jnp.int32),
            pltpu.VMEM(order.shape, jnp.int32),
            *[pltpu.VMEM((rows, width), F32)] * 5,
            pltpu.VMEM(trig.shape, F32),
            halo, halo, halo, halo,
            pltpu.VMEM((angles, width), F32),
            pltpu.VMEM((angles, width), F32),
            pltpu.VMEM((local_f, 5, angles, width), F32),
            pltpu.VMEM((local_f, 5, angles, width), F32),
            pltpu.VMEM((rows, 5, angles, width), F32),
            pltpu.VMEM((rows, angles, width), F32),
            pltpu.VMEM((rows, angles + 4, width), F32),
            pltpu.VMEM((groups * CHUNK, rows * width), F32),
            pltpu.VMEM((devices_all * padded, rows * width), BF16),
            pltpu.VMEM((groups, devices_all * padded, CHUNK), F32),
            pltpu.VMEM((groups, halves, tiles * padded, CHUNK), F32),
            pltpu.VMEM((5, angles, points), F32),
            pltpu.VMEM(((total_f + 4) * pitch, points), F32),
            pltpu.SemaphoreType.DMA(((groups + 1) * halves,)),
            pltpu.SemaphoreType.DMA((groups,)),
            pltpu.SemaphoreType.DMA((8,)),
            pltpu.SemaphoreType.DMA((2, groups)),
            pltpu.SemaphoreType.DMA((2, groups)),
            pltpu.SemaphoreType.DMA((groups,)),
            pltpu.SemaphoreType.DMA((groups,)),
        ],
        compiler_params=pltpu.CompilerParams(
            collective_id=0, has_side_effects=True, vmem_limit_bytes=63 * 1024 * 1024
        ),
    )(
        action.reshape(local_f, angles * rows, width), sea_mask, order, grad_x, grad_y,
        shift_rate, wind_speed, wind_dir, trig,
    )
    return shifted * factor


def solution(mesh):
    return jax.shard_map(
        on_device,
        mesh=mesh,
        in_specs=(
            P("comp", None, ("group", "tile"), None),
            P(("group", "tile"), None),
            P(("group", "tile"), None),
            P(("group", "tile"), None),
            P(("group", "tile"), None),
            P(("group", "tile"), None),
            P(("group", "tile"), None),
            P(("group", "tile"), None),
        ),
        out_specs=P(None, None, ("group", "tile", "comp")),
        check_vma=False,
    )
```
